512 devices in a mesh: head: 8 (over x, core), tok: 64 (over z, y).
Axes of the slice: x: 4, y: 4, z: 16, core: 2. Of those that a mesh axis runs over, the one named last changes fastest.
Arguments:
- query_one: bfloat16 [16384, 4096], P(('head', 'tok')), may hold values from -6 to 6
- key_one: bfloat16 [16384, 4096], P(('head', 'tok')), may hold values from -6 to 6
- value_one: bfloat16 [16384, 4096], P(('head', 'tok')), may hold values from -6 to 6
- rate_one: bfloat16 [16384, 8], P(('head', 'tok')), may hold values from 0.099609375 to 1
- query_two: bfloat16 [16384, 4096], P(('head', 'tok')), may hold values from -6 to 6
- w_gate: float32 [8, 512, 512], P('head', 'tok'), may hold values from -0.25 to 0.25
- w_up: float32 [8, 512, 512], P('head', 'tok'), may hold values from -0.25 to 0.25
- w_down: float32 [8, 512, 512], P('head', 'tok'), may hold values from -0.25 to 0.25
- step_size: float32 [8], P('head'), may hold values from 0.02 to 0.08
Outputs:
- out_one: bfloat16 [16384, 4096], P(('head', 'tok'))
- out_two: bfloat16 [16384, 4096], P(('head', 'tok'))
- gate_new: float32 [8, 512, 512], P('head', 'tok')
- up_new: float32 [8, 512, 512], P('head', 'tok')
- down_new: float32 [8, 512, 512], P('head', 'tok')
The draws below stay inside these ranges and needn't reach their ends.
All inputs are finite; a program needn't handle non-finite values.
Results may differ from the reference program's by a relative error of at most 0.011.
Values may be sent and summed in bfloat16 or wider, within the bound.
A program may use at most 64 MiB of HBM per device.

```python
import math
import jax
import jax.numpy as jnp
from jax import lax

H = 8
D = 512
HID = 512
BLOCK = 16384


def level_of(stream_key, extent, pieces, smallest, largest):
    level, own = 1.0, jax.random.fold_in(stream_key, 6)
    for dim, blocks in pieces:
        heights = jnp.exp(jax.random.uniform(jax.random.fold_in(own, dim), (blocks,), jnp.float32, smallest / len(pieces), largest / len(pieces)))
        level = level * jnp.repeat(heights, extent[dim] // blocks).reshape([-1 if axis == dim else 1 for axis in range(len(extent))])
    return level


def noise(own_key, shape, deviation, reach, pieces=(), kind=jnp.bfloat16):
    entries = jax.random.normal(own_key, shape, jnp.float32) * deviation
    if len(pieces) > 0:
        entries = level_of(own_key, shape, pieces, -0.22, 0.18) * entries
    return jnp.clip(entries, min=-reach, max=reach).astype(kind)


def setup_inputs(seed: int = 0) -> dict:
    seeds = jax.random.split(jax.random.key(seed), 10)
    query_one = noise(seeds[0], (BLOCK, H * D), 1.0, 6.0, ((0, 512),))
    key_one = noise(seeds[1], (BLOCK, H * D), 1.0, 6.0, ((0, 512),))
    value_one = noise(seeds[2], (BLOCK, H * D), 1.0, 6.0, ((0, 512),))
    rate_one = jnp.clip(jnp.exp(math.log(1.0) - 2.306499 * jax.random.uniform(seeds[3], (BLOCK, H), jnp.float32) ** level_of(seeds[3], (BLOCK, H), ((0, 512),), -0.2, 0.2)), 0.099609375, 1.0).astype(jnp.bfloat16)
    query_two = noise(seeds[4], (BLOCK, H * D), 1.0, 6.0, ((0, 512),))
    w_gate = noise(seeds[5], (H, HID, D), D ** -0.5, 0.25, ((0, 8), (1, 64)), jnp.float32)
    w_up = noise(seeds[6], (H, HID, D), D ** -0.5, 0.25, ((0, 8), (1, 64)), jnp.float32)
    w_down = noise(seeds[7], (H, HID, D), HID ** -0.5, 0.25, ((0, 8), (1, 64)), jnp.float32)
    step_size = jnp.clip(jnp.exp(math.log(0.08) - 1.3862944 * jax.random.uniform(seeds[8], (H,), jnp.float32) ** level_of(seeds[8], (H,), ((0, 8),), -0.2, 0.2)), 0.02, 0.08)
    return dict(query_one=query_one, key_one=key_one, value_one=value_one, rate_one=rate_one, query_two=query_two, w_gate=w_gate, w_up=w_up, w_down=w_down, step_size=step_size)


def swiglu_apply(query, gate_b, up_b, down_b):
    pre_gate = jnp.dot(query, gate_b.T, preferred_element_type=jnp.float32)
    pre_up = jnp.dot(query, up_b.T, preferred_element_type=jnp.float32)
    hidden = (pre_gate * jax.nn.sigmoid(pre_gate) * pre_up).astype(jnp.bfloat16)
    return jnp.dot(hidden, down_b, preferred_element_type=jnp.float32)

def renew(weights, grads, step):
    scale = jnp.sqrt(lax.optimization_barrier(jnp.mean(grads * grads, axis=1, keepdims=True)) + 1e-06)
    return weights - step * grads / scale

def head_step(inputs):
    query_a, keys, values, rates, query_b, gate_w, up_w, down_w, step = inputs
    gate_b = gate_w.astype(jnp.bfloat16)
    up_b = up_w.astype(jnp.bfloat16)
    down_b = down_w.astype(jnp.bfloat16)
    first_out = swiglu_apply(query_a, gate_b, up_b, down_b).astype(jnp.bfloat16)
    targets = (-(rates.astype(jnp.float32)[:, None] * values.astype(jnp.float32))).astype(jnp.bfloat16)
    key_gate = jnp.dot(keys, gate_b.T, preferred_element_type=jnp.float32)
    key_up = jnp.dot(keys, up_b.T, preferred_element_type=jnp.float32)
    sigmoid_k = jax.nn.sigmoid(key_gate)
    act_k = key_gate * sigmoid_k
    hidden_k = (act_k * key_up).astype(jnp.bfloat16)
    back = jnp.dot(targets, down_b.T, preferred_element_type=jnp.float32)
    grad_gate_pre = (back * key_up * sigmoid_k * (1.0 + key_gate * (1.0 - sigmoid_k))).astype(jnp.bfloat16)
    grad_up_pre = (back * act_k).astype(jnp.bfloat16)
    grad_gate = jnp.dot(grad_gate_pre.T, keys, preferred_element_type=jnp.float32)
    grad_up = jnp.dot(grad_up_pre.T, keys, preferred_element_type=jnp.float32)
    grad_down = jnp.dot(hidden_k.T, targets, preferred_element_type=jnp.float32)
    gate_next = renew(gate_w, grad_gate, step)
    up_next = renew(up_w, grad_up, step)
    down_next = renew(down_w, grad_down, step)
    second_out = swiglu_apply(query_b, gate_next.astype(jnp.bfloat16), up_next.astype(jnp.bfloat16), down_next.astype(jnp.bfloat16)).astype(jnp.bfloat16)
    return (first_out, second_out, gate_next, up_next, down_next)

def reference(query_one, key_one, value_one, rate_one, query_two, w_gate, w_up, w_down, step_size):

    def by_head(array):
        return array.reshape(BLOCK, H, D).transpose(1, 0, 2)
    first_out, second_out, gate_next, up_next, down_next = lax.map(head_step, (by_head(query_one), by_head(key_one), by_head(value_one), rate_one.T, by_head(query_two), w_gate, w_up, w_down, step_size))

    def merge_heads(array):
        return array.transpose(1, 0, 2).reshape(BLOCK, H * D)
    return (merge_heads(first_out), merge_heads(second_out), gate_next, up_next, down_next)
```

```python
import functools

import jax
import jax.numpy as jnp
from jax import lax
from jax.experimental import pallas as pl
from jax.experimental.pallas import tpu as pltpu
from jax.sharding import PartitionSpec as P

MESH = pl.DeviceIdType.MESH
F32 = jnp.float32
BF16 = jnp.bfloat16
WIDTH = 512
COPIES = 96


def dot_nt(a, b):
    return lax.dot_general(a, b, (((1,), (1,)), ((), ())), preferred_element_type=F32)


def dot_nn(a, b):
    return lax.dot_general(a, b, (((1,), (0,)), ((), ())), preferred_element_type=F32)


def kernel(
    step_ref,
    query_one,
    key_one,
    value_one,
    rate_one,
    query_two,
    w_gate,
    w_up,
    w_down,
    out_one,
    out_two,
    gate_new,
    up_new,
    down_new,
    shard,
    shard_in,
    weights,
    moved,
    negated,
    back_one,
    back_two,
    sums,
    wide_in,
    narrow,
    narrow_in,
    last,
    last_in,
    send_sem,
    recv_sem,
    own_sem,
):
    head = lax.axis_index("head")
    tok = lax.axis_index("tok")
    y = lax.rem(tok, 4)
    z = lax.div(tok, 4)
    low = lax.rem(z, 4)
    high = lax.div(z, 4)

    def at_z(distance):
        return (head, lax.rem(z + 16 + distance, 16) * 4 + y)

    def at_y(distance):
        return (head, z * 4 + lax.rem(y + distance, 4))

    def at_head(distance):
        return (lax.rem(head + distance, 8), tok)

    peers = (
        [at_head(i) for i in range(1, 8)]
        + [at_y(i) for i in range(1, 4)]
        + [at_z(i) for i in (1, -1, 2, -2, 4, 8, 12)]
    )
    count = [0]
    sent = []

    def send(src, dst, peer):
        slot = count[0]
        count[0] += 1
        copy = pltpu.make_async_remote_copy(
            src_ref=src,
            dst_ref=dst,
            send_sem=send_sem.at[slot],
            recv_sem=recv_sem.at[slot],
            device_id=peer,
            device_id_type=MESH,
        )
        copy.start()
        sent.append(copy)
        return copy

    def arrive(copies):
        for copy in copies:
            copy.wait_recv()

    def columns(ref, owner):
        return ref.at[:, pl.ds(pl.multiple_of(owner * WIDTH, WIDTH), WIDTH)]

    def spread(ref, which):
        return [
            send(
                columns(ref, lax.rem(head + i, 8)),
                moved.at[which, head],
                at_head(i),
            )
            for i in range(1, 8)
        ]

    def gather_far(g):
        return [send(shard.at[g], shard_in.at[g, j - 1], at_z(4 * j)) for j in (1, 2, 3)]

    def place(g, value, owner_high):
        part = lax.div(owner_high, 2)
        first = jnp.where(part == 0, y, low)
        second = jnp.where(part == 0, low, y)

        @pl.when(lax.rem(owner_high, 2) == 0)
        def _():
            weights[g, part, first, second, :, 0:8, :] = value

        @pl.when(lax.rem(owner_high, 2) == 1)
        def _():
            weights[g, part, first, second, :, 8:16, :] = value

    def gather_rest(g, far):
        place(g, shard[g], high)
        for j in (1, 2, 3):
            far[j - 1].wait_recv()
            place(g, shard_in[g, j - 1], lax.rem(high + 4 - j, 4))
        a = weights.at[g, 0, y, low]
        c = weights.at[g, 1, low, y]
        a2 = [
            send(a, a, at_z(1)),
            send(a, a, at_z(-1)),
            send(a.at[:, :, 0:256], a.at[:, :, 0:256], at_z(2)),
            send(a.at[:, :, 256:512], a.at[:, :, 256:512], at_z(-2)),
        ]
        c2 = [send(c, c, at_y(i)) for i in (1, 2, 3)]
        arrive(a2)
        a = weights.at[g, 0, y]
        a3 = [send(a, a, at_y(i)) for i in (1, 2, 3)]
        arrive(c2)
        c = weights.at[g, 1, low]
        c3 = [
            send(c, c, at_z(1)),
            send(c, c, at_z(-1)),
            send(c.at[0:2], c.at[0:2], at_z(2)),
            send(c.at[2:4], c.at[2:4], at_z(-2)),
        ]
        return a3, c3

    def matrix(g, part, which):
        return weights[g, part, :, :, which].reshape(256, WIDTH)

    def tokens(which):
        return moved[which].reshape(256, WIDTH)

    def hidden_of(query, g, part):
        pre_gate = dot_nt(query, matrix(g, part, 0))
        pre_up = dot_nt(query, matrix(g, part, 1))
        return (pre_gate * jax.nn.sigmoid(pre_gate) * pre_up).astype(BF16)

    def apply(which, g, result):
        query = tokens(which)
        total = dot_nn(hidden_of(query, g, 0), matrix(g, 0, 2))
        total += dot_nn(hidden_of(query, g, 1), matrix(g, 1, 2))
        result[...] = total.astype(BF16).reshape(8, 32, WIDTH)

    def give_back(result, out):
        copies = [
            send(result.at[lax.rem(head + i, 8)], columns(out, head), at_head(i))
            for i in range(1, 8)
        ]
        own = pltpu.make_async_copy(result.at[head], columns(out, head), own_sem)
        own.start()
        own.wait()
        return copies

    shard[0, 0] = w_gate[0].astype(BF16)
    shard[0, 1] = w_up[0].astype(BF16)
    shard[0, 2] = w_down[0].astype(BF16)

    barrier = pltpu.get_barrier_semaphore()
    for peer in peers:
        pl.semaphore_signal(barrier, inc=1, device_id=peer, device_id_type=MESH)
    pl.semaphore_wait(barrier, len(peers))

    far = gather_far(0)
    keys_in = spread(key_one, 0)
    for h in range(8):
        block = pl.ds(h * WIDTH, WIDTH)
        rate = rate_one[:, h : h + 1].astype(F32)
        negated[:, block] = (-(rate * value_one[:, block].astype(F32))).astype(BF16)
    targets_in = spread(negated, 1)
    mine = pl.ds(pl.multiple_of(head * WIDTH, WIDTH), WIDTH)
    moved[0, head] = key_one[:, mine]
    moved[1, head] = negated[:, mine]
    moved[2, head] = query_one[:, mine]
    moved[3, head] = query_two[:, mine]

    a3, c3 = gather_rest(0, far)
    arrive(keys_in)
    arrive(targets_in)
    query_one_in = spread(query_one, 2)
    query_two_in = spread(query_two, 3)

    def gradients(part):
        keys, targets = tokens(0), tokens(1)
        gate, up, down = (matrix(0, part, i) for i in range(3))
        key_gate = dot_nt(gate, keys)
        key_up = dot_nt(up, keys)
        back = dot_nt(down, targets)
        sig = jax.nn.sigmoid(key_gate)
        act = key_gate * sig
        hidden = (act * key_up).astype(BF16)
        gate_pre = (back * key_up * sig * (1.0 + key_gate * (1.0 - sig))).astype(BF16)
        up_pre = (back * act).astype(BF16)
        for which, (left, right) in enumerate(
            ((gate_pre, keys), (up_pre, keys), (hidden, targets))
        ):
            total = dot_nn(left, right).astype(BF16)
            sums[part, :, :, which] = total.reshape(4, 4, 16, WIDTH)

    arrive(a3)
    gradients(0)
    a1 = [
        send(sums.at[0, lax.rem(y + i, 4)], wide_in.at[0, i - 1], at_y(i)) for i in (1, 2, 3)
    ]
    arrive(c3)
    gradients(1)

    def near(src, dst, split):
        ahead, behind, across = (lax.rem(low + i, 4) for i in (1, 3, 2))
        return [
            send(src.at[ahead], dst.at[0], at_z(1)),
            send(src.at[behind], dst.at[1], at_z(-1)),
            send(split(src.at[across], 0), split(dst.at[2], 0), at_z(2)),
            send(split(src.at[across], 1), split(dst.at[2], 1), at_z(-2)),
        ]

    c1 = near(sums.at[1], wide_in.at[1], lambda ref, i: ref.at[pl.ds(2 * i, 2)])

    arrive(query_one_in)
    apply(2, 0, back_one)
    one_out = give_back(back_one, out_one)

    def add_wide(part, own):
        for i in range(4):
            total = sums[part, own, i].astype(F32)
            for j in range(3):
                total += wide_in[part, j, i].astype(F32)
            narrow[part, i] = total.astype(BF16)

    arrive(a1)
    add_wide(0, y)
    a2 = near(
        narrow.at[0], narrow_in.at[0], lambda ref, i: ref.at[:, :, pl.ds(256 * i, 256)]
    )
    arrive(c1)
    add_wide(1, low)
    c2 = [
        send(narrow.at[1, lax.rem(y + i, 4)], narrow_in.at[1, i - 1], at_y(i))
        for i in (1, 2, 3)
    ]

    def add_narrow(part, own):
        total = narrow[part, own].astype(F32)
        for j in range(3):
            total += narrow_in[part, j].astype(F32)
        last[2 * part] = total[:, 0:8].astype(BF16)
        last[2 * part + 1] = total[:, 8:16].astype(BF16)

    arrive(a2)
    add_narrow(0, low)
    arrive(c2)
    add_narrow(1, y)
    final = [
        send(last.at[lax.rem(high + j, 4)], last_in.at[j - 1], at_z(4 * j)) for j in (1, 2, 3)
    ]
    total = last[high].astype(F32)
    arrive(final)
    for j in range(3):
        total += last_in[j].astype(F32)

    step = step_ref[0]
    for which, (old, new) in enumerate(
        ((w_gate, gate_new), (w_up, up_new), (w_down, down_new))
    ):
        grads = total[which]
        scale = jnp.sqrt(jnp.mean(grads * grads, axis=1, keepdims=True) + 1e-06)
        renewed = old[0] - step * grads / scale
        new[0] = renewed
        shard[1, which] = renewed.astype(BF16)

    far = gather_far(1)
    a3, c3 = gather_rest(1, far)
    arrive(query_two_in)
    arrive(a3)
    arrive(c3)
    apply(3, 1, back_two)
    two_out = give_back(back_two, out_two)
    arrive(one_out)
    arrive(two_out)
    for copy in sent:
        copy.wait_send()


def local(query_one, key_one, value_one, rate_one, query_two, w_gate, w_up, w_down, step_size):
    vmem = pl.BlockSpec(memory_space=pltpu.VMEM)
    smem = pl.BlockSpec(memory_space=pltpu.SMEM)
    hbm = pl.BlockSpec(memory_space=pl.ANY)
    wide = (4, 3, 16, WIDTH)
    return pl.pallas_call(
        kernel,
        out_shape=(
            jax.ShapeDtypeStruct(query_one.shape, BF16),
            jax.ShapeDtypeStruct(query_one.shape, BF16),
            jax.ShapeDtypeStruct(w_gate.shape, F32),
            jax.ShapeDtypeStruct(w_gate.shape, F32),
            jax.ShapeDtypeStruct(w_gate.shape, F32),
        ),
        in_specs=[smem] + [vmem] * 8,
        out_specs=(vmem,) * 5,
        scratch_shapes=[
            pltpu.VMEM((2, 3, 8, WIDTH), BF16),
            pltpu.VMEM((2, 3, 3, 8, WIDTH), BF16),
            pltpu.VMEM((2, 2, 4) + wide, BF16),
            pltpu.VMEM((4, 8, 32, WIDTH), BF16),
            pltpu.VMEM((32, 8 * WIDTH), BF16),
            pltpu.VMEM((8, 32, WIDTH), BF16),
            pltpu.VMEM((8, 32, WIDTH), BF16),
            pltpu.VMEM((2, 4) + wide, BF16),
            pltpu.VMEM((2, 3) + wide, BF16),
            pltpu.VMEM((2,) + wide, BF16),
            pltpu.VMEM((2, 3, 3, 16, WIDTH), BF16),
            pltpu.VMEM((4, 3, 8, WIDTH), BF16),
            pltpu.VMEM((3, 3, 8, WIDTH), BF16),
            pltpu.SemaphoreType.DMA((COPIES,)),
            pltpu.SemaphoreType.DMA((COPIES,)),
            pltpu.SemaphoreType.DMA,
        ],
        compiler_params=pltpu.CompilerParams(
            collective_id=0, has_side_effects=True, vmem_limit_bytes=48 * 1024 * 1024
        ),
        cost_estimate=pl.CostEstimate(
            flops=1700000000, bytes_accessed=2000000, transcendentals=400000
        ),
    )(step_size, query_one, key_one, value_one, rate_one, query_two, w_gate, w_up, w_down)


def solution(mesh):
    rows = P(("head", "tok"), None)
    shards = P("head", "tok", None)
    return jax.shard_map(
        local,
        mesh=mesh,
        in_specs=(rows,) * 5 + (shards,) * 3 + (P("head"),),
        out_specs=(rows,) * 2 + (shards,) * 3,
        check_vma=False,
    )
```

```python
import jax
import jax.numpy as jnp
from jax import lax
from jax.experimental import pallas as pl
from jax.experimental.pallas import tpu as pltpu
from jax.sharding import PartitionSpec as P

MESH = pl.DeviceIdType.MESH
F32 = jnp.float32
BF16 = jnp.bfloat16
WIDTH = 512
COPIES = 128
PAIRS = ((0, 2), (1, 3))


def dot_nt(a, b):
    return lax.dot_general(a, b, (((1,), (1,)), ((), ())), preferred_element_type=F32)


def dot_nn(a, b):
    return lax.dot_general(a, b, (((1,), (0,)), ((), ())), preferred_element_type=F32)


def kernel(
    step_ref,
    rate_turned,
    query_one,
    key_one,
    value_hbm,
    query_two,
    w_gate_hbm,
    w_up_hbm,
    w_down_hbm,
    out_one,
    out_two,
    gate_new,
    up_new,
    down_new,
    value_one,
    w_own,
    fresh,
    shard,
    shard_in,
    near_in,
    weights,
    moved,
    negated,
    back_one,
    back_two,
    sums,
    wide_in,
    narrow,
    narrow_in,
    last,
    last_in,
    send_sem,
    recv_sem,
    load_sem,
    own_sem,
):
    head = lax.axis_index("head")
    tok = lax.axis_index("tok")
    y = lax.rem(tok, 4)
    z = lax.div(tok, 4)
    low = lax.rem(z, 4)
    high = lax.div(z, 4)

    def tok_z(distance):
        return lax.rem(z + 16 + distance, 16) * 4 + y

    def tok_y(distance):
        return z * 4 + lax.rem(y + distance, 4)

    def at_head(distance):
        return (lax.rem(head + distance, 8), tok)

    def tok_near(distance, u):
        if distance == 2:
            return tok_z(jnp.where(lax.rem(u, 2) == 0, 2, -2))
        return tok_z(1 if distance == 1 else -1)

    def pick(u, a, b):
        if isinstance(u, int):
            return a if u < 2 else b
        return jnp.where(u < 2, a, b)

    def peer_two(distance, u):
        return (head, pick(u, tok_near(distance, u), tok_y(distance)))

    def peer_three(distance, u):
        return (head, pick(u, tok_y(distance), tok_near(distance, u)))

    def first(u):
        return pick(u, y, low)

    def second(u):
        return pick(u, low, y)

    sent = []
    count = [0]

    def block_of_slots(size):
        base = count[0]
        count[0] += size
        return base

    def send(slot, src, dst, peer):
        copy = pltpu.make_async_remote_copy(
            src_ref=src,
            dst_ref=dst,
            send_sem=send_sem.at[slot],
            recv_sem=recv_sem.at[slot],
            device_id=peer,
            device_id_type=MESH,
        )
        copy.start()
        sent.append(copy)
        return copy

    def arrive(copies):
        for copy in copies:
            copy.wait_recv()

    def columns(ref, owner):
        return ref.at[:, pl.ds(pl.multiple_of(owner * WIDTH, WIDTH), WIDTH)]

    def spread(ref, which):
        base = block_of_slots(7)
        return [
            send(base + i - 1, columns(ref, lax.rem(head + i, 8)), moved.at[which, head], at_head(i))
            for i in range(1, 8)
        ]

    def place(g, u, other, value):
        for half in range(2):

            @pl.when(lax.rem(other, 2) == half)
            def _():
                rows = slice(8 * half, 8 * half + 8)
                weights[g, u, first(u), lax.div(other, 2), :, rows, :] = value

    units = [lax.rem(high + 4 - j, 4) for j in (0, 3, 1, 2)]

    def gather(g):
        far_base, two_base, three_base = block_of_slots(3), block_of_slots(12), block_of_slots(12)
        far = {
            j: send(far_base + j - 1, shard.at[g], shard_in.at[g, j - 1], (head, tok_z(4 * j)))
            for j in (2, 1, 3)
        }
        two = []
        for n, j in enumerate((0, 3, 1, 2)):
            u = units[n]
            if j:
                far[j].wait_recv()
            block = shard_in.at[g, j - 1] if j else shard.at[g]
            two.append(
                [
                    send(two_base + u * 3 + d - 1, block, near_in.at[g, u, d - 1], peer_two(d, u))
                    for d in (1, 3, 2)
                ]
            )
            place(g, u, second(u), block[...])
        for n in range(4):
            u = units[n]
            arrive(two[n])
            for d in (1, 2, 3):
                place(g, u, lax.rem(second(u) + 4 - d, 4), near_in[g, u, d - 1])
            block = weights.at[g, u, first(u)]
            for d in (1, 3, 2):
                send(three_base + u * 3 + d - 1, block, block, peer_three(d, u))
        return {
            u: [
                pltpu.make_async_remote_copy(
                    src_ref=weights.at[g, u, first(u)],
                    dst_ref=weights.at[g, u, first(u)],
                    send_sem=send_sem.at[three_base + u * 3 + d - 1],
                    recv_sem=recv_sem.at[three_base + u * 3 + d - 1],
                    device_id=peer_three(d, u),
                    device_id_type=MESH,
                )
                for d in (1, 3, 2)
            ]
            for u in range(4)
        }

    def matrix(g, pair, which):
        return jnp.concatenate(
            [weights[g, u, :, :, which].reshape(128, WIDTH) for u in PAIRS[pair]]
        )

    def tokens(which):
        return moved[which].reshape(256, WIDTH)

    def apply(query, g, pair):
        pre_gate = dot_nt(query, matrix(g, pair, 0))
        pre_up = dot_nt(query, matrix(g, pair, 1))
        hidden = (pre_gate * jax.nn.sigmoid(pre_gate) * pre_up).astype(BF16)
        return dot_nn(hidden, matrix(g, pair, 2))

    def give_back(total, result, out, which):
        result[...] = total.astype(BF16).reshape(8, 32, WIDTH)
        base = block_of_slots(7)
        copies = [
            send(base + i - 1, result.at[lax.rem(head + i, 8)], columns(out, head), at_head(i))
            for i in range(1, 8)
        ]
        own = pltpu.make_async_copy(result.at[head], columns(out, head), own_sem.at[which])
        own.start()
        return copies, own

    loads = [
        pltpu.make_async_copy(src, dst, load_sem.at[i])
        for i, (src, dst) in enumerate(
            (
                (w_gate_hbm.at[0], w_own.at[0]),
                (w_up_hbm.at[0], w_own.at[1]),
                (w_down_hbm.at[0], w_own.at[2]),
                (value_hbm, value_one),
                (columns(key_one, head), moved.at[0, head]),
                (columns(query_one, head), moved.at[2, head]),
                (columns(query_two, head), moved.at[3, head]),
            )
        )
    ]
    for load in loads:
        load.start()

    barrier = pltpu.get_barrier_semaphore()
    peers = [(head, tok_z(i)) for i in (8, 4, 12, 2, -2, 1, -1)]
    peers += [(head, tok_y(i)) for i in (2, 1, 3)]
    peers += [at_head(i) for i in range(1, 8)]
    for peer in peers:
        pl.semaphore_signal(barrier, inc=1, device_id=peer, device_id_type=MESH)
    for load in loads:
        load.wait()
    shard[0] = w_own[...].astype(BF16)
    rates = rate_turned[...].astype(F32).T
    for h in range(8):
        block = pl.ds(h * WIDTH, WIDTH)
        product = rates[:, h : h + 1] * value_one[:, block].astype(F32)
        negated[:, block] = (-product).astype(BF16)
    moved[1, head] = negated[:, pl.ds(pl.multiple_of(head * WIDTH, WIDTH), WIDTH)]
    pl.semaphore_wait(barrier, len(peers))

    keys_in = spread(key_one, 0)
    targets_in = spread(negated, 1)
    gathered = gather(0)
    arrive(keys_in)
    arrive(targets_in)

    def gradients(pair):
        keys, targets = tokens(0), tokens(1)
        gate, up, down = (matrix(0, pair, i) for i in range(3))
        key_gate = dot_nt(gate, keys)
        key_up = dot_nt(up, keys)
        back = dot_nt(down, targets)
        sig = jax.nn.sigmoid(key_gate)
        act = key_gate * sig
        hidden = (act * key_up).astype(BF16)
        gate_pre = (back * key_up * sig * (1.0 + key_gate * (1.0 - sig))).astype(BF16)
        up_pre = (back * act).astype(BF16)
        for which, (left, right) in enumerate(
            ((gate_pre, keys), (up_pre, keys), (hidden, targets))
        ):
            total = dot_nn(left, right).astype(BF16)
            for i in range(2):
                part = total[128 * i : 128 * i + 128].reshape(4, 2, 16, WIDTH)
                sums[PAIRS[pair][i], :, :, which] = part

    one_base, two_base, far_base = block_of_slots(12), block_of_slots(12), block_of_slots(3)
    wide, thin = {}, {}

    def send_wide(u):
        wide[u] = [
            send(
                one_base + u * 3 + d - 1,
                sums.at[u, lax.rem(first(u) + d, 4)],
                wide_in.at[u, d - 1],
                peer_three(d, u),
            )
            for d in (1, 3, 2)
        ]

    def send_thin(u):
        arrive(wide[u])
        for i in range(2):
            total = sums[u, first(u), i].astype(F32)
            for d in range(3):
                total += wide_in[u, d, i].astype(F32)
            narrow[u, 2 * i] = total[:, 0:8].astype(BF16)
            narrow[u, 2 * i + 1] = total[:, 8:16].astype(BF16)
        thin[u] = [
            send(
                two_base + u * 3 + d - 1,
                narrow.at[u, lax.rem(second(u) + d, 4)],
                narrow_in.at[u, d - 1],
                peer_two(d, u),
            )
            for d in (1, 3, 2)
        ]

    def send_last(u):
        arrive(thin[u])
        total = narrow[u, second(u)].astype(F32)
        for d in range(3):
            total += narrow_in[u, d].astype(F32)
        last[u] = total.astype(BF16)
        distance = lax.rem(u + 4 - high, 4)

        @pl.when(distance > 0)
        def _():
            far_copy(u, distance).start()

    def far_copy(u, distance):
        slot = far_base + jnp.maximum(distance, 1) - 1
        return pltpu.make_async_remote_copy(
            src_ref=last.at[u],
            dst_ref=last_in.at[jnp.maximum(distance, 1) - 1],
            send_sem=send_sem.at[slot],
            recv_sem=recv_sem.at[slot],
            device_id=(head, lax.rem(z + 4 * distance, 16) * 4 + y),
            device_id_type=MESH,
        )

    for pair in range(2):
        for u in PAIRS[pair]:
            arrive(gathered[u])
        gradients(pair)
        for u in PAIRS[pair]:
            send_wide(u)
    query_one_in = spread(query_one, 2)
    query_two_in = spread(query_two, 3)
    for u in PAIRS[0]:
        send_thin(u)
    for u in PAIRS[0]:
        send_last(u)
    for u in PAIRS[1]:
        send_thin(u)
    for u in PAIRS[1]:
        send_last(u)
    arrive(query_one_in)
    answer = apply(tokens(2), 0, 0) + apply(tokens(2), 0, 1)
    one_out, one_own = give_back(answer, back_one, out_one, 0)
    total = last[high].astype(F32)
    for j in (1, 3, 2):
        far_copy(lax.rem(high + j, 4), j).wait_recv()
        far_copy(lax.rem(high + j, 4), j).wait_send()
        total += last_in[j - 1].astype(F32)

    step = step_ref[0]
    keep = []
    for which, new in enumerate((gate_new, up_new, down_new)):
        grads = total[which]
        scale = jnp.sqrt(jnp.mean(grads * grads, axis=1, keepdims=True) + 1e-06)
        renewed = w_own[which] - step * grads / scale
        fresh[which] = renewed
        keep.append(pltpu.make_async_copy(fresh.at[which], new.at[0], own_sem.at[which + 2]))
        keep[-1].start()
        shard[1, which] = renewed.astype(BF16)

    gathered = gather(1)
    arrive(query_two_in)
    arrive(gathered[0] + gathered[2])
    answer = apply(tokens(3), 1, 0)
    arrive(gathered[1] + gathered[3])
    answer += apply(tokens(3), 1, 1)
    two_out, two_own = give_back(answer, back_two, out_two, 1)
    for copy in [one_own] + keep + [two_own]:
        copy.wait()
    arrive(one_out)
    arrive(two_out)
    for copy in sent:
        copy.wait_send()


def write_out(*refs):
    sources, targets, held = refs[:5], refs[5:10], refs[10:15]
    sems = refs[15]
    into = [pltpu.make_async_copy(sources[i], held[i], sems.at[0, i]) for i in range(5)]
    out = [pltpu.make_async_copy(held[i], targets[i], sems.at[1, i]) for i in range(5)]
    for copy in into:
        copy.start()
    for i in range(5):
        into[i].wait()
        out[i].start()
    for copy in out:
        copy.wait()


def local(query_one, key_one, value_one, rate_one, query_two, w_gate, w_up, w_down, step_size):
    vmem = pl.BlockSpec(memory_space=pltpu.VMEM)
    smem = pl.BlockSpec(memory_space=pltpu.SMEM)
    hbm = pl.BlockSpec(memory_space=pltpu.HBM)
    whole = (2, 3, 16, WIDTH)
    results = (
        jax.ShapeDtypeStruct(query_one.shape, BF16),
        jax.ShapeDtypeStruct(query_one.shape, BF16),
        jax.ShapeDtypeStruct(w_gate.shape, F32),
        jax.ShapeDtypeStruct(w_gate.shape, F32),
        jax.ShapeDtypeStruct(w_gate.shape, F32),
    )
    made = pl.pallas_call(
        kernel,
        out_shape=results,
        in_specs=[smem, vmem] + [hbm] * 7,
        out_specs=(hbm,) * 5,
        scratch_shapes=[
            pltpu.VMEM((32, 8 * WIDTH), BF16),
            pltpu.VMEM((3, 8, WIDTH), F32),
            pltpu.VMEM((3, 8, WIDTH), F32),
            pltpu.VMEM((2, 3, 8, WIDTH), BF16),
            pltpu.VMEM((2, 3, 3, 8, WIDTH), BF16),
            pltpu.VMEM((2, 4, 3, 3, 8, WIDTH), BF16),
            pltpu.VMEM((2, 4, 4) + whole, BF16),
            pltpu.VMEM((4, 8, 32, WIDTH), BF16),
            pltpu.VMEM((32, 8 * WIDTH), BF16),
            pltpu.VMEM((8, 32, WIDTH), BF16),
            pltpu.VMEM((8, 32, WIDTH), BF16),
            pltpu.VMEM((4, 4) + whole, BF16),
            pltpu.VMEM((4, 3) + whole, BF16),
            pltpu.VMEM((4, 4, 3, 8, WIDTH), BF16),
            pltpu.VMEM((4, 3, 3, 8, WIDTH), BF16),
            pltpu.VMEM((4, 3, 8, WIDTH), BF16),
            pltpu.VMEM((3, 3, 8, WIDTH), BF16),
            pltpu.SemaphoreType.DMA((COPIES,)),
            pltpu.SemaphoreType.DMA((COPIES,)),
            pltpu.SemaphoreType.DMA((7,)),
            pltpu.SemaphoreType.DMA((5,)),
        ],
        compiler_params=pltpu.CompilerParams(
            collective_id=0, has_side_effects=True, vmem_limit_bytes=62 * 1024 * 1024
        ),
        cost_estimate=pl.CostEstimate(
            flops=1700000000, bytes_accessed=2000000, transcendentals=400000
        ),
    )(step_size, rate_one.T, query_one, key_one, value_one, query_two, w_gate, w_up, w_down)
    return pl.pallas_call(
        write_out,
        out_shape=results,
        in_specs=[hbm] * 5,
        out_specs=(hbm,) * 5,
        scratch_shapes=[pltpu.VMEM(made[i].shape, made[i].dtype) for i in range(5)]
        + [pltpu.SemaphoreType.DMA((2, 5))],
        compiler_params=pltpu.CompilerParams(vmem_limit_bytes=62 * 1024 * 1024),
    )(*made)


def solution(mesh):
    rows = P(("head", "tok"), None)
    shards = P("head", "tok", None)
    return jax.shard_map(
        local,
        mesh=mesh,
        in_specs=(rows,) * 5 + (shards,) * 3 + (P("head"),),
        out_specs=(rows,) * 2 + (shards,) * 3,
        check_vma=False,
    )
```

```python
import jax
import jax.numpy as jnp
from jax import lax
from jax.experimental import pallas as pl
from jax.experimental.pallas import tpu as pltpu
from jax.sharding import PartitionSpec as P

MESH = pl.DeviceIdType.MESH
F32 = jnp.float32
BF16 = jnp.bfloat16
WIDTH = 512
COPIES = 136
PAIRS = ((0, 2), (1, 3))


def dot_nt(a, b):
    return lax.dot_general(a, b, (((1,), (1,)), ((), ())), preferred_element_type=F32)


def dot_nn(a, b):
    return lax.dot_general(a, b, (((1,), (0,)), ((), ())), preferred_element_type=F32)


def kernel(
    step_hbm,
    rate_hbm,
    query_one,
    key_one,
    value_hbm,
    query_two,
    w_gate_hbm,
    w_up_hbm,
    w_down_hbm,
    out_one,
    out_two,
    gate_new,
    up_new,
    down_new,
    step_ref,
    rate_turned,
    value_one,
    w_own,
    fresh,
    shard,
    shard_in,
    near_in,
    weights,
    moved,
    negated,
    partial,
    partial_in,
    back,
    sums,
    wide_in,
    narrow,
    narrow_in,
    last,
    last_in,
    send_sem,
    recv_sem,
    load_sem,
    own_sem,
):
    row = lax.axis_index("head")
    tok = lax.axis_index("tok")
    core = lax.rem(row, 2)
    y = lax.rem(tok, 4)
    z = lax.div(tok, 4)
    low, high = lax.rem(z, 4), lax.div(z, 4)
    odd, upper = lax.rem(y, 2), lax.div(y, 2)
    head = row - core + odd
    same = core == odd
    other = core != odd
    owner_y = jnp.where(same, y, y + 1 - 2 * odd)

    def tok_z(distance):
        return lax.rem(z + 16 + distance, 16) * 4 + y

    def near(distance, u):
        if distance == 2:
            return (row, tok_z(jnp.where(lax.rem(u, 2) == 0, 2, -2)))
        return (row, tok_z(1 if distance == 1 else -1))

    across = (row, z * 4 + lax.rem(y + 2, 4))
    sibling = (row + 1 - 2 * core, tok)

    def far(j):
        return (head, lax.rem(z + 4 * j, 16) * 4 + owner_y)

    def at_source(h):
        return (lax.div(h, 2) * 2 + core, z * 4 + upper * 2 + lax.rem(h, 2))

    count = [0]
    ends = []

    def slots(size):
        base = count[0]
        count[0] += size
        return base

    def remote(slot, src, dst, peer):
        return pltpu.make_async_remote_copy(
            src_ref=src,
            dst_ref=dst,
            send_sem=send_sem.at[slot],
            recv_sem=recv_sem.at[slot],
            device_id=peer,
            device_id_type=MESH,
        )

    def send(slot, src, dst, peer):
        copy = remote(slot, src, dst, peer)
        copy.start()
        ends.append(copy)
        return copy

    def arrive(copies):
        for copy in copies:
            copy.wait_recv()

    def columns(ref, h):
        return ref.at[:, pl.ds(pl.multiple_of(h * WIDTH, WIDTH), WIDTH)]

    def spread(ref, which):
        base = slots(7)
        copies = []
        for i in range(1, 8):
            h = lax.rem(head + i, 8)
            copies.append(
                send(base + i - 1, columns(ref, h), moved.at[which, core, head], at_source(h))
            )
        return copies

    def share(copies, which):
        arrive(copies)
        half = moved.at[which, core]
        return [send(slots(1), half, half, sibling)]

    def place(g, u, k, half, value):
        for i in range(2):

            @pl.when(half == i)
            def _():
                weights[g, u, k, :, 8 * i : 8 * i + 8, :] = value

    units = [lax.rem(high + 4 - j, 4) for j in (0, 3, 1, 2)]
    bases = [(slots(4), slots(12), slots(12)) for _ in range(2)]

    def copy_far(g, j):
        return remote(bases[g][0] + j, shard.at[g], shard_in.at[g, j], far(j))

    def copies_two(g, u, j, along_z):
        base = bases[g][1] + u * 3
        block = shard_in.at[g, j]
        if along_z:
            return [
                remote(base + d - 1, block, near_in.at[g, u, d - 1], near(d, u))
                for d in (1, 3, 2)
            ]
        return [remote(base, block, near_in.at[g, u, 0], across)]

    def copies_three(g, u, along_z):
        base = bases[g][2] + u * 3
        if along_z:
            block = weights.at[g, u, low]
            return [remote(base + d - 1, block, block, near(d, u)) for d in (1, 3, 2)]
        block = weights.at[g, u, pl.ds(upper * 2, 2)]
        return [remote(base, block, block, across)]

    def gather_start(g):
        for j in (2, 1, 3):
            copy_far(g, j).start()

        @pl.when(other)
        def _():
            copy_far(g, 0).start()

        @pl.when(same)
        def _():
            shard_in[g, 0] = shard[g]

    def gather_two(g):
        for n, j in enumerate((0, 3, 1, 2)):
            u = units[n]
            if j:
                copy_far(g, j).wait_recv()
            else:

                @pl.when(other)
                def _():
                    copy_far(g, 0).wait_recv()

            @pl.when(u < 2)
            def _():
                for copy in copies_two(g, u, j, True):
                    copy.start()
                place(g, u, upper * 2 + lax.div(low, 2), lax.rem(low, 2), shard_in[g, j])

            @pl.when(u >= 2)
            def _():
                for copy in copies_two(g, u, j, False):
                    copy.start()
                place(g, u, low, upper, shard_in[g, j])

    def gather_three(g):
        for n, j in enumerate((0, 3, 1, 2)):
            u = units[n]

            @pl.when(u < 2)
            def _():
                arrive(copies_two(g, u, j, True))
                for d in (1, 2, 3):
                    s = lax.rem(low + 4 - d, 4)
                    k = upper * 2 + lax.div(s, 2)
                    place(g, u, k, lax.rem(s, 2), near_in[g, u, d - 1])
                for copy in copies_three(g, u, False):
                    copy.start()

            @pl.when(u >= 2)
            def _():
                arrive(copies_two(g, u, j, False))
                place(g, u, low, 1 - upper, near_in[g, u, 0])
                for copy in copies_three(g, u, True):
                    copy.start()

    def gathered(g, u):
        arrive(copies_three(g, u, u >= 2))

    def gather_end(g):
        for j in (1, 2, 3):
            copy_far(g, j).wait_send()

        @pl.when(other)
        def _():
            copy_far(g, 0).wait_send()

        for u in range(4):
            for copy in copies_two(g, u, 0, u < 2) + copies_three(g, u, u >= 2):
                copy.wait_send()

    def matrix(g, chosen, which):
        return jnp.concatenate([weights[g, u, :, which].reshape(64, WIDTH) for u in chosen])

    def apply(which, g, slot, out):
        gate, up, down = (matrix(g, range(4), i) for i in range(3))

        def part(half):
            query = moved[which, half].reshape(256, WIDTH)
            pre_gate = dot_nt(query, gate)
            pre_up = dot_nt(query, up)
            hidden = (pre_gate * jax.nn.sigmoid(pre_gate) * pre_up).astype(BF16)
            return dot_nn(hidden, down)

        partial[slot] = part(1 - core).astype(BF16).reshape(8, 32, WIDTH)
        exchange = send(slots(1), partial.at[slot], partial_in.at[slot], sibling)
        total = part(core)
        exchange.wait_recv()
        total += partial_in[slot].reshape(256, WIDTH).astype(F32)
        back[slot] = total.astype(BF16).reshape(8, 32, WIDTH)
        base = slots(7)
        copies = []
        for i in range(1, 8):
            h = lax.rem(head + i, 8)
            copies.append(
                send(base + i - 1, back.at[slot, h], columns(out, head), at_source(h))
            )
        own = pltpu.make_async_copy(back.at[slot, head], columns(out, head), own_sem.at[slot])
        own.start()
        return copies, own

    loads = [
        pltpu.make_async_copy(src, dst, load_sem.at[i])
        for i, (src, dst) in enumerate(
            (
                (w_gate_hbm.at[0], w_own.at[0]),
                (w_up_hbm.at[0], w_own.at[1]),
                (w_down_hbm.at[0], w_own.at[2]),
                (value_hbm, value_one),
                (rate_hbm, rate_turned),
                (step_hbm, step_ref),
                (columns(key_one, head), moved.at[0, core, head]),
                (columns(query_one, head), moved.at[2, core, head]),
                (columns(query_two, head), moved.at[3, core, head]),
            )
        )
    ]
    for load in loads:
        load.start()

    barrier = pltpu.get_barrier_semaphore()
    peers = [far(2), far(1), far(3)]
    peers += [(row, tok_z(i)) for i in (2, -2, 1, -1)] + [across, sibling]
    peers += [at_source(lax.rem(head + i, 8)) for i in range(1, 8)]
    for peer in peers:
        pl.semaphore_signal(barrier, inc=1, device_id=peer, device_id_type=MESH)

    @pl.when(other)
    def _():
        pl.semaphore_signal(barrier, inc=1, device_id=far(0), device_id_type=MESH)

    for load in loads[:3]:
        load.wait()
    shard[0] = w_own[...].astype(BF16)
    pl.semaphore_wait(barrier, len(peers) + jnp.where(same, 0, 1))

    gather_start(0)
    keys_in = spread(key_one, 0)
    for load in loads[3:]:
        load.wait()
    rates = rate_turned[...].astype(F32).T
    for h in range(8):
        block = pl.ds(h * WIDTH, WIDTH)
        product = rates[:, h : h + 1] * value_one[:, block].astype(F32)
        negated[:, block] = (-product).astype(BF16)
    targets_in = spread(negated, 1)
    moved[1, core, head] = negated[:, pl.ds(pl.multiple_of(head * WIDTH, WIDTH), WIDTH)]
    gather_two(0)
    keys_shared = share(keys_in, 0)
    targets_shared = share(targets_in, 1)
    gather_three(0)
    arrive(keys_shared)
    arrive(targets_shared)

    def gradients(chosen):
        keys, targets = moved[0].reshape(512, WIDTH), moved[1].reshape(512, WIDTH)
        gate, up, down = (matrix(0, chosen, i) for i in range(3))
        key_gate = dot_nt(gate, keys)
        key_up = dot_nt(up, keys)
        back_prod = dot_nt(down, targets)
        sig = jax.nn.sigmoid(key_gate)
        act = key_gate * sig
        hidden = (act * key_up).astype(BF16)
        gate_pre = (back_prod * key_up * sig * (1.0 + key_gate * (1.0 - sig))).astype(BF16)
        up_pre = (back_prod * act).astype(BF16)
        for which, (left, right) in enumerate(
            ((gate_pre, keys), (up_pre, keys), (hidden, targets))
        ):
            total = dot_nn(left, right).astype(BF16)
            for i, u in enumerate(chosen):
                sums[u, :, which] = total[64 * i : 64 * i + 64].reshape(4, 16, WIDTH)

    one_base, two_base, far_base = slots(12), slots(12), slots(4)
    wide, thin = {}, {}

    def send_wide(u):
        base = one_base + u * 3
        if u < 2:
            there = sums.at[u, pl.ds((1 - upper) * 2, 2)]
            wide[u] = [send(base, there, wide_in.at[u, pl.ds(0, 2)], across)]
        else:
            wide[u] = [
                send(
                    base + d - 1, sums.at[u, lax.rem(low + d, 4)], wide_in.at[u, d - 1], near(d, u)
                )
                for d in (1, 3, 2)
            ]

    def send_thin(u):
        arrive(wide[u])
        base = two_base + u * 3
        if u < 2:
            for i in range(2):
                total = sums[u, upper * 2 + i].astype(F32) + wide_in[u, i].astype(F32)
                narrow[u, 2 * i] = total[:, 0:8].astype(BF16)
                narrow[u, 2 * i + 1] = total[:, 8:16].astype(BF16)
            thin[u] = [
                send(
                    base + d - 1,
                    narrow.at[u, lax.rem(low + d, 4)],
                    narrow_in.at[u, d - 1],
                    near(d, u),
                )
                for d in (1, 3, 2)
            ]
        else:
            total = sums[u, low].astype(F32)
            for d in range(3):
                total += wide_in[u, d].astype(F32)
            narrow[u, 0] = total[:, 0:8].astype(BF16)
            narrow[u, 1] = total[:, 8:16].astype(BF16)
            thin[u] = [send(base, narrow.at[u, 1 - upper], narrow_in.at[u, 0], across)]

    def copy_last(u, j):
        return remote(far_base + j, last.at[u], last_in.at[j], far(j))

    def send_last(u):
        arrive(thin[u])
        if u < 2:
            total = narrow[u, low].astype(F32)
            for d in range(3):
                total += narrow_in[u, d].astype(F32)
        else:
            total = narrow[u, upper].astype(F32) + narrow_in[u, 0].astype(F32)
        last[u] = total.astype(BF16)
        j = lax.rem(u + 4 - high, 4)
        home = (j == 0) & same

        @pl.when(home)
        def _():
            last_in[0] = total.astype(BF16)

        @pl.when(jnp.logical_not(home))
        def _():
            copy_last(u, j).start()

    for chosen in PAIRS:
        for u in chosen:
            gathered(0, u)
        gradients(chosen)
        for u in chosen:
            send_wide(u)
    for u in PAIRS[0]:
        send_thin(u)
    for u in PAIRS[0]:
        send_last(u)
    for u in PAIRS[1]:
        send_thin(u)
    for u in PAIRS[1]:
        send_last(u)

    query_one_in = spread(query_one, 2)
    query_two_in = spread(query_two, 3)

    @pl.when(other)
    def _():
        copy_last(high, 0).wait_recv()

    total = last_in[0].astype(F32)
    for j in (1, 3, 2):
        copy_last(lax.rem(high + j, 4), j).wait_recv()
        total += last_in[j].astype(F32)

    step = step_ref[0]
    keep = []
    for which, new in enumerate((gate_new, up_new, down_new)):
        grads = total[which]
        scale = jnp.sqrt(jnp.mean(grads * grads, axis=1, keepdims=True) + 1e-06)
        renewed = w_own[which] - step * grads / scale
        fresh[which] = renewed
        keep.append(pltpu.make_async_copy(fresh.at[which], new.at[0], own_sem.at[which + 2]))
        keep[-1].start()
        shard[1, which] = renewed.astype(BF16)

    gather_start(1)
    one_shared = share(query_one_in, 2)
    two_shared = share(query_two_in, 3)
    arrive(one_shared)
    one_out, one_own = apply(2, 0, 0, out_one)
    gather_two(1)
    gather_three(1)
    arrive(two_shared)
    for u in range(4):
        gathered(1, u)
    two_out, two_own = apply(3, 1, 1, out_two)
    for copy in [one_own] + keep + [two_own]:
        copy.wait()
    arrive(one_out)
    for j in (1, 2, 3):
        copy_last(lax.rem(high + j, 4), j).wait_send()

    @pl.when(other)
    def _():
        copy_last(high, 0).wait_send()

    gather_end(0)
    gather_end(1)
    arrive(two_out)
    for copy in ends:
        copy.wait_send()


def write_out(*refs):
    sources, targets, held = refs[:5], refs[5:10], refs[10:15]
    sems = refs[15]
    into = [pltpu.make_async_copy(sources[i], held[i], sems.at[0, i]) for i in range(5)]
    out = [pltpu.make_async_copy(held[i], targets[i], sems.at[1, i]) for i in range(5)]
    for copy in into:
        copy.start()
    for i in range(5):
        into[i].wait()
        out[i].start()
    for copy in out:
        copy.wait()


def local(query_one, key_one, value_one, rate_one, query_two, w_gate, w_up, w_down, step_size):
    hbm = pl.BlockSpec(memory_space=pltpu.HBM)
    results = (
        jax.ShapeDtypeStruct(query_one.shape, BF16),
        jax.ShapeDtypeStruct(query_one.shape, BF16),
        jax.ShapeDtypeStruct(w_gate.shape, F32),
        jax.ShapeDtypeStruct(w_gate.shape, F32),
        jax.ShapeDtypeStruct(w_gate.shape, F32),
    )
    made = pl.pallas_call(
        kernel,
        out_shape=results,
        in_specs=[hbm] * 9,
        out_specs=(hbm,) * 5,
        scratch_shapes=[
            pltpu.SMEM((1,), F32),
            pltpu.VMEM((8, 32), BF16),
            pltpu.VMEM((32, 8 * WIDTH), BF16),
            pltpu.VMEM((3, 8, WIDTH), F32),
            pltpu.VMEM((3, 8, WIDTH), F32),
            pltpu.VMEM((2, 3, 8, WIDTH), BF16),
            pltpu.VMEM((2, 4, 3, 8, WIDTH), BF16),
            pltpu.VMEM((2, 4, 3, 3, 8, WIDTH), BF16),
            pltpu.VMEM((2, 4, 4, 3, 16, WIDTH), BF16),
            pltpu.VMEM((4, 2, 8, 32, WIDTH), BF16),
            pltpu.VMEM((32, 8 * WIDTH), BF16),
            pltpu.VMEM((2, 8, 32, WIDTH), BF16),
            pltpu.VMEM((2, 8, 32, WIDTH), BF16),
            pltpu.VMEM((2, 8, 32, WIDTH), BF16),
            pltpu.VMEM((4, 4, 3, 16, WIDTH), BF16),
            pltpu.VMEM((4, 3, 3, 16, WIDTH), BF16),
            pltpu.VMEM((4, 4, 3, 8, WIDTH), BF16),
            pltpu.VMEM((4, 3, 3, 8, WIDTH), BF16),
            pltpu.VMEM((4, 3, 8, WIDTH), BF16),
            pltpu.VMEM((4, 3, 8, WIDTH), BF16),
            pltpu.SemaphoreType.DMA((COPIES,)),
            pltpu.SemaphoreType.DMA((COPIES,)),
            pltpu.SemaphoreType.DMA((9,)),
            pltpu.SemaphoreType.DMA((5,)),
        ],
        compiler_params=pltpu.CompilerParams(
            collective_id=0, has_side_effects=True, vmem_limit_bytes=62 * 1024 * 1024
        ),
        cost_estimate=pl.CostEstimate(
            flops=1700000000, bytes_accessed=2000000, transcendentals=400000
        ),
    )(step_size, rate_one.T, query_one, key_one, value_one, query_two, w_gate, w_up, w_down)
    return pl.pallas_call(
        write_out,
        out_shape=results,
        in_specs=[hbm] * 5,
        out_specs=(hbm,) * 5,
        scratch_shapes=[pltpu.VMEM(made[i].shape, made[i].dtype) for i in range(5)]
        + [pltpu.SemaphoreType.DMA((2, 5))],
        compiler_params=pltpu.CompilerParams(vmem_limit_bytes=62 * 1024 * 1024),
    )(*made)


def solution(mesh):
    rows = P(("head", "tok"), None)
    shards = P("head", "tok", None)
    return jax.shard_map(
        local,
        mesh=mesh,
        in_specs=(rows,) * 5 + (shards,) * 3 + (P("head"),),
        out_specs=(rows,) * 2 + (shards,) * 3,
        check_vma=False,
    )
```

```python
import jax
import jax.numpy as jnp
from jax import lax
from jax.experimental import pallas as pl
from jax.experimental.pallas import tpu as pltpu
from jax.sharding import PartitionSpec as P

MESH = pl.DeviceIdType.MESH
F32 = jnp.float32
BF16 = jnp.bfloat16
WIDTH = 512
COPIES = 136
PAIRS = ((0, 2), (1, 3))


def dot_nt(a, b):
    return lax.dot_general(a, b, (((1,), (1,)), ((), ())), preferred_element_type=F32)


def dot_nn(a, b):
    return lax.dot_general(a, b, (((1,), (0,)), ((), ())), preferred_element_type=F32)


def kernel(
    step_hbm,
    rate_hbm,
    query_one,
    key_one,
    value_hbm,
    query_two,
    w_gate_hbm,
    w_up_hbm,
    w_down_hbm,
    out_one,
    out_two,
    gate_new,
    up_new,
    down_new,
    step_ref,
    rate_turned,
    value_one,
    w_own,
    fresh,
    shard,
    shard_in,
    near_in,
    weights,
    moved,
    negated,
    partial,
    partial_in,
    back,
    sums,
    wide_in,
    narrow,
    narrow_in,
    last,
    last_in,
    send_sem,
    recv_sem,
    load_sem,
    own_sem,
):
    row = lax.axis_index("head")
    tok = lax.axis_index("tok")
    core = lax.rem(row, 2)
    y = lax.rem(tok, 4)
    z = lax.div(tok, 4)
    low, high = lax.rem(z, 4), lax.div(z, 4)
    odd, upper = lax.rem(y, 2), lax.div(y, 2)
    head = row - core + odd
    same = core == odd
    other = core != odd
    owner_y = jnp.where(same, y, y + 1 - 2 * odd)

    def tok_z(distance):
        return lax.rem(z + 16 + distance, 16) * 4 + y

    def near(distance, u):
        if distance == 2:
            return (row, tok_z(jnp.where(lax.rem(u, 2) == 0, 2, -2)))
        return (row, tok_z(1 if distance == 1 else -1))

    across = (row, z * 4 + lax.rem(y + 2, 4))
    sibling = (row + 1 - 2 * core, tok)

    def far(j):
        return (head, lax.rem(z + 4 * j, 16) * 4 + owner_y)

    def at_source(h):
        return (lax.div(h, 2) * 2 + core, z * 4 + upper * 2 + lax.rem(h, 2))

    count = [0]
    ends = []

    def slots(size):
        base = count[0]
        count[0] += size
        return base

    def remote(slot, src, dst, peer):
        return pltpu.make_async_remote_copy(
            src_ref=src,
            dst_ref=dst,
            send_sem=send_sem.at[slot],
            recv_sem=recv_sem.at[slot],
            device_id=peer,
            device_id_type=MESH,
        )

    def send(slot, src, dst, peer):
        copy = remote(slot, src, dst, peer)
        copy.start()
        ends.append(copy)
        return copy

    def arrive(copies):
        for copy in copies:
            copy.wait_recv()

    def columns(ref, h):
        return ref.at[:, pl.ds(pl.multiple_of(h * WIDTH, WIDTH), WIDTH)]

    def spread(ref, which):
        base = slots(7)
        copies = []
        for i in range(1, 8):
            h = lax.rem(head + i, 8)
            copies.append(
                send(base + i - 1, columns(ref, h), moved.at[which, core, head], at_source(h))
            )
        return copies

    def share(copies, which):
        arrive(copies)
        half = moved.at[which, core]
        return [send(slots(1), half, half, sibling)]

    def place(g, u, k, half, value):
        for i in range(2):

            @pl.when(half == i)
            def _():
                weights[g, u, k, :, 8 * i : 8 * i + 8, :] = value

    units = [lax.rem(high + 4 - j, 4) for j in (0, 3, 1, 2)]
    bases = [(slots(4), slots(12), slots(12)) for _ in range(2)]

    def copy_far(g, j):
        return remote(bases[g][0] + j, shard.at[g], shard_in.at[g, j], far(j))

    def copies_two(g, u, j, along_z):
        base = bases[g][1] + u * 3
        block = shard_in.at[g, j]
        if along_z:
            return [
                remote(base + d - 1, block, near_in.at[g, u, d - 1], near(d, u))
                for d in (1, 3, 2)
            ]
        return [remote(base, block, near_in.at[g, u, 0], across)]

    def copies_three(g, u, along_z):
        base = bases[g][2] + u * 3
        if along_z:
            block = weights.at[g, u, low]
            return [remote(base + d - 1, block, block, near(d, u)) for d in (1, 3, 2)]
        block = weights.at[g, u, pl.ds(upper * 2, 2)]
        return [remote(base, block, block, across)]

    def gather_start(g):
        for j in (2, 1, 3):
            copy_far(g, j).start()

        @pl.when(other)
        def _():
            copy_far(g, 0).start()

        @pl.when(same)
        def _():
            shard_in[g, 0] = shard[g]

    def gather_two(g):
        for n, j in enumerate((0, 3, 1, 2)):
            u = units[n]
            if j:
                copy_far(g, j).wait_recv()
            else:

                @pl.when(other)
                def _():
                    copy_far(g, 0).wait_recv()

            @pl.when(u < 2)
            def _():
                for copy in copies_two(g, u, j, True):
                    copy.start()
                place(g, u, upper * 2 + lax.div(low, 2), lax.rem(low, 2), shard_in[g, j])

            @pl.when(u >= 2)
            def _():
                for copy in copies_two(g, u, j, False):
                    copy.start()
                place(g, u, low, upper, shard_in[g, j])

    def gather_three(g):
        for n, j in enumerate((0, 3, 1, 2)):
            u = units[n]

            @pl.when(u < 2)
            def _():
                arrive(copies_two(g, u, j, True))
                for d in (1, 2, 3):
                    s = lax.rem(low + 4 - d, 4)
                    k = upper * 2 + lax.div(s, 2)
                    place(g, u, k, lax.rem(s, 2), near_in[g, u, d - 1])
                for copy in copies_three(g, u, False):
                    copy.start()

            @pl.when(u >= 2)
            def _():
                arrive(copies_two(g, u, j, False))
                place(g, u, low, 1 - upper, near_in[g, u, 0])
                for copy in copies_three(g, u, True):
                    copy.start()

    def gathered(g, u):
        arrive(copies_three(g, u, u >= 2))

    def gather_end(g):
        for j in (1, 2, 3):
            copy_far(g, j).wait_send()

        @pl.when(other)
        def _():
            copy_far(g, 0).wait_send()

        for u in range(4):
            for copy in copies_two(g, u, 0, u < 2) + copies_three(g, u, u >= 2):
                copy.wait_send()

    def matrix(g, chosen, which):
        return jnp.concatenate([weights[g, u, :, which].reshape(64, WIDTH) for u in chosen])

    def apply(which, g, slot, out):
        gate, up, down = (matrix(g, range(4), i) for i in range(3))

        def part(half):
            query = moved[which, half].reshape(256, WIDTH)
            pre_gate = dot_nt(query, gate)
            pre_up = dot_nt(query, up)
            hidden = (pre_gate * jax.nn.sigmoid(pre_gate) * pre_up).astype(BF16)
            return dot_nn(hidden, down)

        partial[slot] = part(1 - core).astype(BF16).reshape(8, 32, WIDTH)
        exchange = send(slots(1), partial.at[slot], partial_in.at[slot], sibling)
        total = part(core)
        exchange.wait_recv()
        total += partial_in[slot].reshape(256, WIDTH).astype(F32)
        back[slot] = total.astype(BF16).reshape(8, 32, WIDTH)
        base = slots(7)
        copies = []
        for i in range(1, 8):
            h = lax.rem(head + i, 8)
            copies.append(
                send(base + i - 1, back.at[slot, h], columns(out, head), at_source(h))
            )
        own = pltpu.make_async_copy(back.at[slot, head], columns(out, head), own_sem.at[slot])
        own.start()
        return copies, own

    loads = [
        pltpu.make_async_copy(src, dst, load_sem.at[i])
        for i, (src, dst) in enumerate(
            (
                (w_gate_hbm.at[0], w_own.at[0]),
                (w_up_hbm.at[0], w_own.at[1]),
                (w_down_hbm.at[0], w_own.at[2]),
                (value_hbm, value_one),
                (rate_hbm, rate_turned),
                (step_hbm, step_ref),
                (columns(key_one, head), moved.at[0, core, head]),
                (columns(query_one, head), moved.at[2, core, head]),
                (columns(query_two, head), moved.at[3, core, head]),
            )
        )
    ]
    for load in loads:
        load.start()

    barrier = pltpu.get_barrier_semaphore()
    peers = [far(2), far(1), far(3)]
    peers += [(row, tok_z(i)) for i in (2, -2, 1, -1)] + [across, sibling]
    peers += [at_source(lax.rem(head + i, 8)) for i in range(1, 8)]
    for peer in peers:
        pl.semaphore_signal(barrier, inc=1, device_id=peer, device_id_type=MESH)

    @pl.when(other)
    def _():
        pl.semaphore_signal(barrier, inc=1, device_id=far(0), device_id_type=MESH)

    for load in loads[:3]:
        load.wait()
    shard[0] = w_own[...].astype(BF16)
    pl.semaphore_wait(barrier, len(peers) + jnp.where(same, 0, 1))

    gather_start(0)
    keys_in = spread(key_one, 0)
    for load in loads[3:]:
        load.wait()
    rates = rate_turned[...].astype(F32).T
    for h in range(8):
        block = pl.ds(h * WIDTH, WIDTH)
        product = rates[:, h : h + 1] * value_one[:, block].astype(F32)
        negated[:, block] = (-product).astype(BF16)
    targets_in = spread(negated, 1)
    moved[1, core, head] = negated[:, pl.ds(pl.multiple_of(head * WIDTH, WIDTH), WIDTH)]
    gather_two(0)
    keys_shared = share(keys_in, 0)
    targets_shared = share(targets_in, 1)
    gather_three(0)
    query_one_in = spread(query_one, 2)
    arrive(keys_shared)
    arrive(targets_shared)

    def gradients(chosen):
        keys, targets = moved[0].reshape(512, WIDTH), moved[1].reshape(512, WIDTH)
        gate, up, down = (matrix(0, chosen, i) for i in range(3))
        key_gate = dot_nt(gate, keys)
        key_up = dot_nt(up, keys)
        back_prod = dot_nt(down, targets)
        sig = jax.nn.sigmoid(key_gate)
        act = key_gate * sig
        hidden = (act * key_up).astype(BF16)
        gate_pre = (back_prod * key_up * sig * (1.0 + key_gate * (1.0 - sig))).astype(BF16)
        up_pre = (back_prod * act).astype(BF16)
        for which, (left, right) in enumerate(
            ((gate_pre, keys), (up_pre, keys), (hidden, targets))
        ):
            total = dot_nn(left, right).astype(BF16)
            for i, u in enumerate(chosen):
                sums[u, :, which] = total[64 * i : 64 * i + 64].reshape(4, 16, WIDTH)

    one_base, two_base, far_base = slots(12), slots(12), slots(4)
    wide, thin = {}, {}

    def send_wide(u):
        base = one_base + u * 3
        if u < 2:
            there = sums.at[u, pl.ds((1 - upper) * 2, 2)]
            wide[u] = [send(base, there, wide_in.at[u, pl.ds(0, 2)], across)]
        else:
            wide[u] = [
                send(
                    base + d - 1, sums.at[u, lax.rem(low + d, 4)], wide_in.at[u, d - 1], near(d, u)
                )
                for d in (1, 3, 2)
            ]

    def send_thin(u):
        arrive(wide[u])
        base = two_base + u * 3
        if u < 2:
            for i in range(2):
                total = sums[u, upper * 2 + i].astype(F32) + wide_in[u, i].astype(F32)
                narrow[u, 2 * i] = total[:, 0:8].astype(BF16)
                narrow[u, 2 * i + 1] = total[:, 8:16].astype(BF16)
            thin[u] = [
                send(
                    base + d - 1,
                    narrow.at[u, lax.rem(low + d, 4)],
                    narrow_in.at[u, d - 1],
                    near(d, u),
                )
                for d in (1, 3, 2)
            ]
        else:
            total = sums[u, low].astype(F32)
            for d in range(3):
                total += wide_in[u, d].astype(F32)
            narrow[u, 0] = total[:, 0:8].astype(BF16)
            narrow[u, 1] = total[:, 8:16].astype(BF16)
            thin[u] = [send(base, narrow.at[u, 1 - upper], narrow_in.at[u, 0], across)]

    def copy_last(u, j):
        return remote(far_base + j, last.at[u], last_in.at[j], far(j))

    def send_last(u):
        arrive(thin[u])
        if u < 2:
            total = narrow[u, low].astype(F32)
            for d in range(3):
                total += narrow_in[u, d].astype(F32)
        else:
            total = narrow[u, upper].astype(F32) + narrow_in[u, 0].astype(F32)
        last[u] = total.astype(BF16)
        j = lax.rem(u + 4 - high, 4)
        home = (j == 0) & same

        @pl.when(home)
        def _():
            last_in[0] = total.astype(BF16)

        @pl.when(jnp.logical_not(home))
        def _():
            copy_last(u, j).start()

    for chosen in PAIRS:
        for u in chosen:
            gathered(0, u)
        gradients(chosen)
        for u in chosen:
            send_wide(u)
    for u in PAIRS[0]:
        send_thin(u)
    for u in PAIRS[1]:
        send_thin(u)
    one_shared = share(query_one_in, 2)
    for u in PAIRS[0]:
        send_last(u)
    for u in PAIRS[1]:
        send_last(u)

    arrive(one_shared)
    one_out, one_own = apply(2, 0, 0, out_one)

    @pl.when(other)
    def _():
        copy_last(high, 0).wait_recv()

    total = last_in[0].astype(F32)
    for j in (1, 3, 2):
        copy_last(lax.rem(high + j, 4), j).wait_recv()
        total += last_in[j].astype(F32)

    step = step_ref[0]
    keep = []
    for which, new in enumerate((gate_new, up_new, down_new)):
        grads = total[which]
        scale = jnp.sqrt(jnp.mean(grads * grads, axis=1, keepdims=True) + 1e-06)
        renewed = w_own[which] - step * grads / scale
        fresh[which] = renewed
        keep.append(pltpu.make_async_copy(fresh.at[which], new.at[0], own_sem.at[which + 2]))
        keep[-1].start()
        shard[1, which] = renewed.astype(BF16)

    gather_start(1)
    query_two_in = spread(query_two, 3)
    gather_two(1)
    gather_three(1)
    two_shared = share(query_two_in, 3)
    arrive(two_shared)
    for u in range(4):
        gathered(1, u)
    two_out, two_own = apply(3, 1, 1, out_two)
    for copy in [one_own] + keep + [two_own]:
        copy.wait()
    arrive(one_out)
    for j in (1, 2, 3):
        copy_last(lax.rem(high + j, 4), j).wait_send()

    @pl.when(other)
    def _():
        copy_last(high, 0).wait_send()

    gather_end(0)
    gather_end(1)
    arrive(two_out)
    for copy in ends:
        copy.wait_send()


def write_out(*refs):
    sources, targets, held = refs[:5], refs[5:10], refs[10:15]
    sems = refs[15]
    into = [pltpu.make_async_copy(sources[i], held[i], sems.at[0, i]) for i in range(5)]
    out = [pltpu.make_async_copy(held[i], targets[i], sems.at[1, i]) for i in range(5)]
    for copy in into:
        copy.start()
    for i in range(5):
        into[i].wait()
        out[i].start()
    for copy in out:
        copy.wait()


def local(query_one, key_one, value_one, rate_one, query_two, w_gate, w_up, w_down, step_size):
    hbm = pl.BlockSpec(memory_space=pltpu.HBM)
    results = (
        jax.ShapeDtypeStruct(query_one.shape, BF16),
        jax.ShapeDtypeStruct(query_one.shape, BF16),
        jax.ShapeDtypeStruct(w_gate.shape, F32),
        jax.ShapeDtypeStruct(w_gate.shape, F32),
        jax.ShapeDtypeStruct(w_gate.shape, F32),
    )
    made = pl.pallas_call(
        kernel,
        out_shape=results,
        in_specs=[hbm] * 9,
        out_specs=(hbm,) * 5,
        scratch_shapes=[
            pltpu.SMEM((1,), F32),
            pltpu.VMEM((8, 32), BF16),
            pltpu.VMEM((32, 8 * WIDTH), BF16),
            pltpu.VMEM((3, 8, WIDTH), F32),
            pltpu.VMEM((3, 8, WIDTH), F32),
            pltpu.VMEM((2, 3, 8, WIDTH), BF16),
            pltpu.VMEM((2, 4, 3, 8, WIDTH), BF16),
            pltpu.VMEM((2, 4, 3, 3, 8, WIDTH), BF16),
            pltpu.VMEM((2, 4, 4, 3, 16, WIDTH), BF16),
            pltpu.VMEM((4, 2, 8, 32, WIDTH), BF16),
            pltpu.VMEM((32, 8 * WIDTH), BF16),
            pltpu.VMEM((2, 8, 32, WIDTH), BF16),
            pltpu.VMEM((2, 8, 32, WIDTH), BF16),
            pltpu.VMEM((2, 8, 32, WIDTH), BF16),
            pltpu.VMEM((4, 4, 3, 16, WIDTH), BF16),
            pltpu.VMEM((4, 3, 3, 16, WIDTH), BF16),
            pltpu.VMEM((4, 4, 3, 8, WIDTH), BF16),
            pltpu.VMEM((4, 3, 3, 8, WIDTH), BF16),
            pltpu.VMEM((4, 3, 8, WIDTH), BF16),
            pltpu.VMEM((4, 3, 8, WIDTH), BF16),
            pltpu.SemaphoreType.DMA((COPIES,)),
            pltpu.SemaphoreType.DMA((COPIES,)),
            pltpu.SemaphoreType.DMA((9,)),
            pltpu.SemaphoreType.DMA((5,)),
        ],
        compiler_params=pltpu.CompilerParams(
            collective_id=0, has_side_effects=True, vmem_limit_bytes=62 * 1024 * 1024
        ),
        cost_estimate=pl.CostEstimate(
            flops=1700000000, bytes_accessed=2000000, transcendentals=400000
        ),
    )(step_size, rate_one.T, query_one, key_one, value_one, query_two, w_gate, w_up, w_down)
    return pl.pallas_call(
        write_out,
        out_shape=results,
        in_specs=[hbm] * 5,
        out_specs=(hbm,) * 5,
        scratch_shapes=[pltpu.VMEM(made[i].shape, made[i].dtype) for i in range(5)]
        + [pltpu.SemaphoreType.DMA((2, 5))],
        compiler_params=pltpu.CompilerParams(vmem_limit_bytes=62 * 1024 * 1024),
    )(*made)


def solution(mesh):
    rows = P(("head", "tok"), None)
    shards = P("head", "tok", None)
    return jax.shard_map(
        local,
        mesh=mesh,
        in_specs=(rows,) * 5 + (shards,) * 3 + (P("head"),),
        out_specs=(rows,) * 2 + (shards,) * 3,
        check_vma=False,
    )
```

```python
import jax
import jax.numpy as jnp
from jax import lax
from jax.experimental import pallas as pl
from jax.experimental.pallas import tpu as pltpu
from jax.sharding import PartitionSpec as P

MESH = pl.DeviceIdType.MESH
F32 = jnp.float32
BF16 = jnp.bfloat16
WIDTH = 512
COPIES = 136
PAIRS = ((0, 2), (1, 3))


def dot_nt(a, b):
    return lax.dot_general(a, b, (((1,), (1,)), ((), ())), preferred_element_type=F32)


def dot_nn(a, b):
    return lax.dot_general(a, b, (((1,), (0,)), ((), ())), preferred_element_type=F32)


def kernel(
    step_hbm,
    rate_hbm,
    query_one,
    key_one,
    value_hbm,
    query_two,
    w_gate_hbm,
    w_up_hbm,
    w_down_hbm,
    out_one,
    out_two,
    gate_new,
    up_new,
    down_new,
    step_ref,
    rate_turned,
    value_one,
    w_own,
    fresh,
    shard,
    shard_in,
    near_in,
    weights,
    moved,
    negated,
    partial,
    partial_in,
    back,
    sums,
    wide_in,
    narrow,
    narrow_in,
    last,
    last_in,
    send_sem,
    recv_sem,
    load_sem,
    own_sem,
):
    row = lax.axis_index("head")
    tok = lax.axis_index("tok")
    core = lax.rem(row, 2)
    y = lax.rem(tok, 4)
    z = lax.div(tok, 4)
    low, high = lax.rem(z, 4), lax.div(z, 4)
    odd, upper = lax.rem(y, 2), lax.div(y, 2)
    head = row - core + odd
    same = core == odd
    other = core != odd
    owner_y = jnp.where(same, y, y + 1 - 2 * odd)

    def tok_z(distance):
        return lax.rem(z + 16 + distance, 16) * 4 + y

    def near(distance, u):
        if distance == 2:
            return (row, tok_z(jnp.where(lax.rem(u, 2) == 0, 2, -2)))
        return (row, tok_z(1 if distance == 1 else -1))

    across = (row, z * 4 + lax.rem(y + 2, 4))
    sibling = (row + 1 - 2 * core, tok)

    def far(j):
        return (head, lax.rem(z + 4 * j, 16) * 4 + owner_y)

    def at_source(h):
        return (lax.div(h, 2) * 2 + core, z * 4 + upper * 2 + lax.rem(h, 2))

    count = [0]
    ends = []

    def slots(size):
        base = count[0]
        count[0] += size
        return base

    def remote(slot, src, dst, peer):
        return pltpu.make_async_remote_copy(
            src_ref=src,
            dst_ref=dst,
            send_sem=send_sem.at[slot],
            recv_sem=recv_sem.at[slot],
            device_id=peer,
            device_id_type=MESH,
        )

    def send(slot, src, dst, peer):
        copy = remote(slot, src, dst, peer)
        copy.start()
        ends.append(copy)
        return copy

    def arrive(copies):
        for copy in copies:
            copy.wait_recv()

    def columns(ref, h):
        return ref.at[:, pl.ds(pl.multiple_of(h * WIDTH, WIDTH), WIDTH)]

    def spread(ref, which):
        base = slots(7)
        copies = []
        for i in range(1, 8):
            h = lax.rem(head + i, 8)
            copies.append(
                send(base + i - 1, columns(ref, h), moved.at[which, core, head], at_source(h))
            )
        return copies

    def share(copies, which):
        arrive(copies)
        half = moved.at[which, core]
        return [send(slots(1), half, half, sibling)]

    def place(g, u, k, half, value):
        for i in range(2):

            @pl.when(half == i)
            def _():
                weights[g, u, k, :, 8 * i : 8 * i + 8, :] = value

    units = [lax.rem(high + 4 - j, 4) for j in (0, 3, 1, 2)]
    bases = [(slots(4), slots(12), slots(12)) for _ in range(2)]

    def copy_far(g, j):
        return remote(bases[g][0] + j, shard.at[g], shard_in.at[g, j], far(j))

    def copies_two(g, u, j, along_z):
        base = bases[g][1] + u * 3
        block = shard_in.at[g, j]
        if along_z:
            return [
                remote(base + d - 1, block, near_in.at[g, u, d - 1], near(d, u))
                for d in (2, 1, 3)
            ]
        return [remote(base, block, near_in.at[g, u, 0], across)]

    def copies_three(g, u, along_z):
        base = bases[g][2] + u * 3
        if along_z:
            block = weights.at[g, u, low]
            return [remote(base + d - 1, block, block, near(d, u)) for d in (2, 1, 3)]
        block = weights.at[g, u, pl.ds(upper * 2, 2)]
        return [remote(base, block, block, across)]

    def gather_start(g):
        for j in (2, 1, 3):
            copy_far(g, j).start()

        @pl.when(other)
        def _():
            copy_far(g, 0).start()

        @pl.when(same)
        def _():
            shard_in[g, 0] = shard[g]

    def gather_two(g):
        for n, j in enumerate((0, 3, 1, 2)):
            u = units[n]
            if j:
                copy_far(g, j).wait_recv()
            else:

                @pl.when(other)
                def _():
                    copy_far(g, 0).wait_recv()

            @pl.when(u < 2)
            def _():
                for copy in copies_two(g, u, j, True):
                    copy.start()
                place(g, u, upper * 2 + lax.div(low, 2), lax.rem(low, 2), shard_in[g, j])

            @pl.when(u >= 2)
            def _():
                for copy in copies_two(g, u, j, False):
                    copy.start()
                place(g, u, low, upper, shard_in[g, j])

    def gather_three(g):
        for n, j in enumerate((0, 3, 1, 2)):
            u = units[n]

            @pl.when(u < 2)
            def _():
                arrive(copies_two(g, u, j, True))
                for d in (1, 2, 3):
                    s = lax.rem(low + 4 - d, 4)
                    k = upper * 2 + lax.div(s, 2)
                    place(g, u, k, lax.rem(s, 2), near_in[g, u, d - 1])
                for copy in copies_three(g, u, False):
                    copy.start()

            @pl.when(u >= 2)
            def _():
                arrive(copies_two(g, u, j, False))
                place(g, u, low, 1 - upper, near_in[g, u, 0])
                for copy in copies_three(g, u, True):
                    copy.start()

    def gathered(g, u):
        arrive(copies_three(g, u, u >= 2))

    def gather_end(g):
        for j in (1, 2, 3):
            copy_far(g, j).wait_send()

        @pl.when(other)
        def _():
            copy_far(g, 0).wait_send()

        for u in range(4):
            for copy in copies_two(g, u, 0, u < 2) + copies_three(g, u, u >= 2):
                copy.wait_send()

    def matrix(g, chosen, which):
        return jnp.concatenate([weights[g, u, :, which].reshape(64, WIDTH) for u in chosen])

    def apply(which, g, slot, out):
        gate, up, down = (matrix(g, range(4), i) for i in range(3))

        def part(half):
            query = moved[which, half].reshape(256, WIDTH)
            pre_gate = dot_nt(query, gate)
            pre_up = dot_nt(query, up)
            hidden = (pre_gate * jax.nn.sigmoid(pre_gate) * pre_up).astype(BF16)
            return dot_nn(hidden, down)

        partial[slot] = part(1 - core).astype(BF16).reshape(8, 32, WIDTH)
        exchange = send(slots(1), partial.at[slot], partial_in.at[slot], sibling)
        total = part(core)
        exchange.wait_recv()
        total += partial_in[slot].reshape(256, WIDTH).astype(F32)
        back[slot] = total.astype(BF16).reshape(8, 32, WIDTH)
        base = slots(7)
        copies = []
        for i in range(1, 8):
            h = lax.rem(head + i, 8)
            copies.append(
                send(base + i - 1, back.at[slot, h], columns(out, head), at_source(h))
            )
        own = pltpu.make_async_copy(back.at[slot, head], columns(out, head), own_sem.at[slot])
        own.start()
        return copies, own

    loads = [
        pltpu.make_async_copy(src, dst, load_sem.at[i])
        for i, (src, dst) in enumerate(
            (
                (w_gate_hbm.at[0], w_own.at[0]),
                (w_up_hbm.at[0], w_own.at[1]),
                (w_down_hbm.at[0], w_own.at[2]),
                (value_hbm, value_one),
                (rate_hbm, rate_turned),
                (step_hbm, step_ref),
                (columns(key_one, head), moved.at[0, core, head]),
                (columns(query_one, head), moved.at[2, core, head]),
                (columns(query_two, head), moved.at[3, core, head]),
            )
        )
    ]
    for load in loads:
        load.start()

    barrier = pltpu.get_barrier_semaphore()
    peers = [far(2), far(1), far(3)]
    peers += [(row, tok_z(i)) for i in (2, -2, 1, -1)] + [across, sibling]
    peers += [at_source(lax.rem(head + i, 8)) for i in range(1, 8)]
    for peer in peers:
        pl.semaphore_signal(barrier, inc=1, device_id=peer, device_id_type=MESH)

    @pl.when(other)
    def _():
        pl.semaphore_signal(barrier, inc=1, device_id=far(0), device_id_type=MESH)

    for load in loads[:3]:
        load.wait()
    shard[0] = w_own[...].astype(BF16)
    pl.semaphore_wait(barrier, len(peers) + jnp.where(same, 0, 1))

    gather_start(0)
    keys_in = spread(key_one, 0)
    for load in loads[3:]:
        load.wait()
    rates = rate_turned[...].astype(F32).T
    for h in range(8):
        block = pl.ds(h * WIDTH, WIDTH)
        product = rates[:, h : h + 1] * value_one[:, block].astype(F32)
        negated[:, block] = (-product).astype(BF16)
    targets_in = spread(negated, 1)
    moved[1, core, head] = negated[:, pl.ds(pl.multiple_of(head * WIDTH, WIDTH), WIDTH)]
    gather_two(0)
    gather_three(0)
    keys_shared = share(keys_in, 0)
    targets_shared = share(targets_in, 1)
    query_one_in = spread(query_one, 2)
    arrive(keys_shared)
    arrive(targets_shared)

    def gradients(chosen):
        keys, targets = moved[0].reshape(512, WIDTH), moved[1].reshape(512, WIDTH)
        gate, up, down = (matrix(0, chosen, i) for i in range(3))
        key_gate = dot_nt(gate, keys)
        key_up = dot_nt(up, keys)
        back_prod = dot_nt(down, targets)
        sig = jax.nn.sigmoid(key_gate)
        act = key_gate * sig
        hidden = (act * key_up).astype(BF16)
        gate_pre = (back_prod * key_up * sig * (1.0 + key_gate * (1.0 - sig))).astype(BF16)
        up_pre = (back_prod * act).astype(BF16)
        for which, (left, right) in enumerate(
            ((gate_pre, keys), (up_pre, keys), (hidden, targets))
        ):
            total = dot_nn(left, right).astype(BF16)
            for i, u in enumerate(chosen):
                sums[u, :, which] = total[64 * i : 64 * i + 64].reshape(4, 16, WIDTH)

    one_base, two_base, far_base = slots(12), slots(12), slots(4)
    wide, thin = {}, {}

    def send_wide(u):
        base = one_base + u * 3
        if u < 2:
            there = sums.at[u, pl.ds((1 - upper) * 2, 2)]
            wide[u] = [send(base, there, wide_in.at[u, pl.ds(0, 2)], across)]
        else:
            wide[u] = [
                send(
                    base + d - 1, sums.at[u, lax.rem(low + d, 4)], wide_in.at[u, d - 1], near(d, u)
                )
                for d in (2, 1, 3)
            ]

    def send_thin(u):
        arrive(wide[u])
        base = two_base + u * 3
        if u < 2:
            for i in range(2):
                total = sums[u, upper * 2 + i].astype(F32) + wide_in[u, i].astype(F32)
                narrow[u, 2 * i] = total[:, 0:8].astype(BF16)
                narrow[u, 2 * i + 1] = total[:, 8:16].astype(BF16)
            thin[u] = [
                send(
                    base + d - 1,
                    narrow.at[u, lax.rem(low + d, 4)],
                    narrow_in.at[u, d - 1],
                    near(d, u),
                )
                for d in (2, 1, 3)
            ]
        else:
            total = sums[u, low].astype(F32)
            for d in range(3):
                total += wide_in[u, d].astype(F32)
            narrow[u, 0] = total[:, 0:8].astype(BF16)
            narrow[u, 1] = total[:, 8:16].astype(BF16)
            thin[u] = [send(base, narrow.at[u, 1 - upper], narrow_in.at[u, 0], across)]

    def copy_last(u, j):
        return remote(far_base + j, last.at[u], last_in.at[j], far(j))

    def send_last(u):
        arrive(thin[u])
        if u < 2:
            total = narrow[u, low].astype(F32)
            for d in range(3):
                total += narrow_in[u, d].astype(F32)
        else:
            total = narrow[u, upper].astype(F32) + narrow_in[u, 0].astype(F32)
        last[u] = total.astype(BF16)
        j = lax.rem(u + 4 - high, 4)
        home = (j == 0) & same

        @pl.when(home)
        def _():
            last_in[0] = total.astype(BF16)

        @pl.when(jnp.logical_not(home))
        def _():
            copy_last(u, j).start()

    for chosen in PAIRS:
        for u in chosen:
            gathered(0, u)
        gradients(chosen)
        for u in chosen:
            send_wide(u)
    for u in PAIRS[0]:
        send_thin(u)
    for u in PAIRS[1]:
        send_thin(u)
    one_shared = share(query_one_in, 2)
    for u in PAIRS[0]:
        send_last(u)
    for u in PAIRS[1]:
        send_last(u)

    arrive(one_shared)
    one_out, one_own = apply(2, 0, 0, out_one)

    @pl.when(other)
    def _():
        copy_last(high, 0).wait_recv()

    total = last_in[0].astype(F32)
    for j in (1, 3, 2):
        copy_last(lax.rem(high + j, 4), j).wait_recv()
        total += last_in[j].astype(F32)

    step = step_ref[0]
    keep = []
    for which, new in enumerate((gate_new, up_new, down_new)):
        grads = total[which]
        scale = jnp.sqrt(jnp.mean(grads * grads, axis=1, keepdims=True) + 1e-06)
        renewed = w_own[which] - step * grads / scale
        fresh[which] = renewed
        keep.append(pltpu.make_async_copy(fresh.at[which], new.at[0], own_sem.at[which + 2]))
        keep[-1].start()
        shard[1, which] = renewed.astype(BF16)

    gather_start(1)
    query_two_in = spread(query_two, 3)
    gather_two(1)
    gather_three(1)
    two_shared = share(query_two_in, 3)
    arrive(two_shared)
    for u in range(4):
        gathered(1, u)
    two_out, two_own = apply(3, 1, 1, out_two)
    for copy in [one_own] + keep + [two_own]:
        copy.wait()
    arrive(one_out)
    for j in (1, 2, 3):
        copy_last(lax.rem(high + j, 4), j).wait_send()

    @pl.when(other)
    def _():
        copy_last(high, 0).wait_send()

    gather_end(0)
    gather_end(1)
    arrive(two_out)
    for copy in ends:
        copy.wait_send()


def write_out(*refs):
    sources, targets, held = refs[:5], refs[5:10], refs[10:15]
    sems = refs[15]
    into = [pltpu.make_async_copy(sources[i], held[i], sems.at[0, i]) for i in range(5)]
    out = [pltpu.make_async_copy(held[i], targets[i], sems.at[1, i]) for i in range(5)]
    for copy in into:
        copy.start()
    for i in range(5):
        into[i].wait()
        out[i].start()
    for copy in out:
        copy.wait()


def local(query_one, key_one, value_one, rate_one, query_two, w_gate, w_up, w_down, step_size):
    hbm = pl.BlockSpec(memory_space=pltpu.HBM)
    results = (
        jax.ShapeDtypeStruct(query_one.shape, BF16),
        jax.ShapeDtypeStruct(query_one.shape, BF16),
        jax.ShapeDtypeStruct(w_gate.shape, F32),
        jax.ShapeDtypeStruct(w_gate.shape, F32),
        jax.ShapeDtypeStruct(w_gate.shape, F32),
    )
    made = pl.pallas_call(
        kernel,
        out_shape=results,
        in_specs=[hbm] * 9,
        out_specs=(hbm,) * 5,
        scratch_shapes=[
            pltpu.SMEM((1,), F32),
            pltpu.VMEM((8, 32), BF16),
            pltpu.VMEM((32, 8 * WIDTH), BF16),
            pltpu.VMEM((3, 8, WIDTH), F32),
            pltpu.VMEM((3, 8, WIDTH), F32),
            pltpu.VMEM((2, 3, 8, WIDTH), BF16),
            pltpu.VMEM((2, 4, 3, 8, WIDTH), BF16),
            pltpu.VMEM((2, 4, 3, 3, 8, WIDTH), BF16),
            pltpu.VMEM((2, 4, 4, 3, 16, WIDTH), BF16),
            pltpu.VMEM((4, 2, 8, 32, WIDTH), BF16),
            pltpu.VMEM((32, 8 * WIDTH), BF16),
            pltpu.VMEM((2, 8, 32, WIDTH), BF16),
            pltpu.VMEM((2, 8, 32, WIDTH), BF16),
            pltpu.VMEM((2, 8, 32, WIDTH), BF16),
            pltpu.VMEM((4, 4, 3, 16, WIDTH), BF16),
            pltpu.VMEM((4, 3, 3, 16, WIDTH), BF16),
            pltpu.VMEM((4, 4, 3, 8, WIDTH), BF16),
            pltpu.VMEM((4, 3, 3, 8, WIDTH), BF16),
            pltpu.VMEM((4, 3, 8, WIDTH), BF16),
            pltpu.VMEM((4, 3, 8, WIDTH), BF16),
            pltpu.SemaphoreType.DMA((COPIES,)),
            pltpu.SemaphoreType.DMA((COPIES,)),
            pltpu.SemaphoreType.DMA((9,)),
            pltpu.SemaphoreType.DMA((5,)),
        ],
        compiler_params=pltpu.CompilerParams(
            collective_id=0, has_side_effects=True, vmem_limit_bytes=62 * 1024 * 1024
        ),
        cost_estimate=pl.CostEstimate(
            flops=1700000000, bytes_accessed=2000000, transcendentals=400000
        ),
    )(step_size, rate_one.T, query_one, key_one, value_one, query_two, w_gate, w_up, w_down)
    return pl.pallas_call(
        write_out,
        out_shape=results,
        in_specs=[hbm] * 5,
        out_specs=(hbm,) * 5,
        scratch_shapes=[pltpu.VMEM(made[i].shape, made[i].dtype) for i in range(5)]
        + [pltpu.SemaphoreType.DMA((2, 5))],
        compiler_params=pltpu.CompilerParams(vmem_limit_bytes=62 * 1024 * 1024),
    )(*made)


def solution(mesh):
    rows = P(("head", "tok"), None)
    shards = P("head", "tok", None)
    return jax.shard_map(
        local,
        mesh=mesh,
        in_specs=(rows,) * 5 + (shards,) * 3 + (P("head"),),
        out_specs=(rows,) * 2 + (shards,) * 3,
        check_vma=False,
    )
```
